256 devices in a mesh: row: 32 (over y, x, core), col: 8 (over z).
Axes of the slice: x: 4, y: 4, z: 8, core: 2. Of those that a mesh axis runs over, the one named last changes fastest.
Arguments:
- tokens: bfloat16 [256, 8192], P('row', 'col'), may hold values from -6 to 6
- gate_weight: bfloat16 [8192, 28672], P('row', 'col'), may hold values from -0.0625 to 0.0625
- up_weight: bfloat16 [8192, 28672], P('row', 'col'), may hold values from -0.0625 to 0.0625
- down_weight: bfloat16 [28672, 8192], P('row', 'col'), may hold values from -0.03125 to 0.03125
- out_grad: bfloat16 [256, 8192], P('row', 'col'), may hold values from -1.5 to 1.5
Outputs:
- output: bfloat16 [256, 8192], P('row', 'col')
- grad_tokens: bfloat16 [256, 8192], P('row', 'col')
- grad_gate_weight: bfloat16 [8192, 28672], P('row', 'col')
- grad_up_weight: bfloat16 [8192, 28672], P('row', 'col')
- grad_down_weight: bfloat16 [28672, 8192], P('row', 'col')
The draws below stay inside these ranges and needn't reach their ends.
All inputs are finite; a program needn't handle non-finite values.
Results may differ from the reference program's by a relative error of at most 0.04.
Values may be sent and summed in bfloat16 or wider, within the bound.
No kernel may reach another device: no remote copies, remote signals or barrier semaphores. Data moves between devices by JAX's collectives and lax.ppermute only.
A program may use at most 64 MiB of HBM per device.

```python
import jax
import jax.numpy as jnp
from jax import lax

D = 8192
FF = 28672
TOKENS = 256
N_ROW = 32
N_COL = 8


def block_levels(own_key, extent, shards, smallest, largest):
    def one(axis_at, blocks):
        heights = jax.random.uniform(jax.random.fold_in(jax.random.fold_in(own_key, 6), axis_at), (blocks,), jnp.float32, smallest / len(shards), largest / len(shards))
        return jnp.repeat(jnp.exp(heights), extent[axis_at] // blocks).reshape((-1,) + (1,) * (len(extent) - axis_at - 1))

    factor_of = one(*shards[0])
    for cut in shards[1:]:
        factor_of = factor_of * one(*cut)
    return factor_of


def scatter_about(key, shape, spread, most, cuts=(), kind=jnp.bfloat16):
    values = jax.random.normal(key, shape, jnp.float32) * spread
    if len(cuts) > 0:
        values = block_levels(key, shape, cuts, -0.22, 0.18) * values
    return jnp.clip(values, min=-most, max=most).astype(kind)


def setup_inputs(seed: int = 0) -> dict:
    splits = jax.random.split(jax.random.key(seed), 6)
    tokens = scatter_about(splits[0], (TOKENS, D), 1.0, 6.0, ((0, 32), (1, 8)))
    gate_weight = scatter_about(splits[1], (D, FF), D ** -0.5, 0.0625, ((0, 32), (1, 8)))
    up_weight = scatter_about(splits[2], (D, FF), D ** -0.5, 0.0625, ((0, 32), (1, 8)))
    down_weight = scatter_about(splits[3], (FF, D), FF ** -0.5, 0.03125, ((0, 32), (1, 8)))
    out_grad = scatter_about(splits[4], (TOKENS, D), 0.25, 1.5, ((0, 32), (1, 8)))
    return dict(tokens=tokens, gate_weight=gate_weight, up_weight=up_weight, down_weight=down_weight, out_grad=out_grad)


def block_sum(pairs, parts):
    height = pairs[0][0].shape[0]
    across = pairs[0][1].shape[1]
    width = pairs[0][0].shape[1] // parts

    def step(total, index):
        begin = (index * width).astype(jnp.int32)
        term = jnp.zeros((height, across), jnp.float32)
        for left, right in pairs:
            left_block = lax.dynamic_slice_in_dim(left, begin, width, 1).astype(jnp.float32)
            right_block = lax.dynamic_slice_in_dim(right, begin, width, 0).astype(jnp.float32)
            term = term + jnp.dot(left_block, right_block, preferred_element_type=jnp.float32)
        rounded = lax.optimization_barrier(term.astype(jnp.bfloat16))
        return total + rounded.astype(jnp.float32), None

    total, _ = lax.scan(step, jnp.zeros((height, across), jnp.float32), jnp.arange(parts, dtype=jnp.int32))
    return total


def transposed_product(left, right):
    return jnp.dot(left.T.astype(jnp.float32), right.astype(jnp.float32), preferred_element_type=jnp.float32).astype(jnp.bfloat16)


def reference(tokens, gate_weight, up_weight, down_weight, out_grad):
    gate = block_sum([(tokens, gate_weight)], N_ROW)
    up = block_sum([(tokens, up_weight)], N_ROW)
    sigmoid_gate = jax.nn.sigmoid(gate)
    silu_gate = gate * sigmoid_gate
    hidden = (silu_gate * up).astype(jnp.bfloat16)
    output = block_sum([(hidden, down_weight)], N_ROW).astype(jnp.bfloat16)
    grad_down_weight = transposed_product(hidden, out_grad)
    grad_hidden = block_sum([(out_grad, down_weight.T)], N_COL)
    grad_gate = (grad_hidden * up * sigmoid_gate * (1.0 + gate * (1.0 - sigmoid_gate))).astype(jnp.bfloat16)
    grad_up = (grad_hidden * silu_gate).astype(jnp.bfloat16)
    grad_gate_weight = transposed_product(tokens, grad_gate)
    grad_up_weight = transposed_product(tokens, grad_up)
    grad_tokens = block_sum([(grad_gate, gate_weight.T), (grad_up, up_weight.T)], N_COL).astype(jnp.bfloat16)
    return output, grad_tokens, grad_gate_weight, grad_up_weight, grad_down_weight
```

```python
import jax
import jax.numpy as jnp
from jax import lax
from jax.sharding import Mesh, PartitionSpec as P

Y, X, CORES, Z = 4, 4, 2, 8
CHIPS = Y * X
PLANE = ("y", "x")
ROW = ("y", "x", "core")
EVERY = ("y", "x", "core", "z")
SWAP = [(0, 1), (1, 0)]
BF16, F32 = jnp.bfloat16, jnp.float32


def rows_times(left, right):
    return lax.dot_general(left, right, (((1,), (1,)), ((), ())), preferred_element_type=F32)


def columns_times(left, right):
    return lax.dot_general(left, right, (((0,), (0,)), ((), ())), preferred_element_type=F32)


def times(left, right):
    return jnp.dot(left, right, preferred_element_type=F32)


def exchange(blocks, axis):
    return lax.all_to_all(blocks, axis, split_axis=0, concat_axis=0, tiled=True)


def spread(block, axis, count):
    return exchange(jnp.broadcast_to(block[None], (count,) + block.shape), axis)


def total(blocks):
    return jnp.sum(blocks.astype(F32), axis=0)


def unit_routes():
    routes = []
    for flip in range(2):
        route = []
        for chip in range(CHIPS):
            for core in range(CORES):
                for z in range(Z):
                    source = (chip * CORES + core) * Z + z
                    target = ((2 * z + (core ^ flip)) * CORES + chip % 2) * Z + chip // 2
                    route.append((source, target))
        routes.append(route)
    return routes


TO_OWNER = unit_routes()
FROM_OWNER = [[(b, a) for a, b in route] for route in TO_OWNER]


def local(tokens, gate_weight, up_weight, down_weight, out_grad):
    core = lax.axis_index("core")
    odd = lax.axis_index("x") % 2
    mine_tokens, width = tokens.shape
    depth, units = gate_weight.shape
    half = units // 2

    def halves(weight):
        mine = lax.dynamic_slice_in_dim(weight, core * half, half, 1)
        theirs = lax.dynamic_slice_in_dim(weight, (1 - core) * half, half, 1)
        return mine, lax.ppermute(theirs, "core", SWAP)

    gate_mine, gate_got = halves(gate_weight)
    up_mine, up_got = halves(up_weight)

    every_feature = spread(tokens, "z", Z)
    cotangent = spread(out_grad, ROW, CHIPS * CORES).reshape(-1, width)

    hidden_part = rows_times(cotangent, down_weight).astype(BF16)
    hidden_sum = total(exchange(hidden_part.reshape(Z, -1, hidden_part.shape[1]), "z")).astype(BF16)
    sixteen = hidden_sum.shape[0] // 2
    got = [
        lax.ppermute(
            lax.dynamic_slice_in_dim(hidden_sum, (core ^ flip) * sixteen, sixteen, 0),
            EVERY,
            TO_OWNER[flip],
        )
        for flip in range(2)
    ]
    grad_hidden = jnp.where(
        odd == 0, jnp.concatenate(got, 1), jnp.concatenate(got[::-1], 1)
    ).astype(F32)

    features = width * Z // CHIPS
    parts = every_feature.reshape(Z, mine_tokens, 2, features).transpose(0, 2, 1, 3)
    parts = parts.reshape(CHIPS, 1, mine_tokens, features)
    parts = jnp.broadcast_to(parts, (CHIPS, CORES, mine_tokens, features))
    panel = exchange(parts.reshape(CHIPS * CORES, mine_tokens, features), ROW).reshape(-1, features)
    panel_mine = lax.dynamic_slice_in_dim(panel, core * depth, depth, 1)
    panel_other = lax.dynamic_slice_in_dim(panel, (1 - core) * depth, depth, 1)

    gate_part = (times(panel_mine, gate_mine) + times(panel_other, gate_got)).astype(BF16)
    up_part = (times(panel_mine, up_mine) + times(panel_other, up_got)).astype(BF16)
    both = jnp.concatenate([gate_part, up_part], 1).reshape(CHIPS, -1, 2 * half)
    both = total(exchange(both, PLANE))
    gate, up = both[:, :half], both[:, half:]
    sigmoid_gate = jax.nn.sigmoid(gate)
    silu_gate = gate * sigmoid_gate
    hidden = (silu_gate * up).astype(BF16)
    grad_gate = grad_hidden * up * sigmoid_gate * (1.0 + gate * (1.0 - sigmoid_gate))
    grad_up = grad_hidden * silu_gate
    grads = jnp.concatenate([grad_gate.astype(BF16), grad_up.astype(BF16)], 1)

    quarter = half // 2
    got = [
        lax.ppermute(
            lax.dynamic_slice_in_dim(hidden, (odd ^ flip) * quarter, quarter, 1),
            EVERY,
            FROM_OWNER[flip],
        )
        for flip in range(2)
    ]
    hidden_rows = jnp.where(core == 0, jnp.concatenate(got, 0), jnp.concatenate(got[::-1], 0))

    pieces = spread(grads, PLANE, CHIPS).reshape(-1, 2 * half)
    hidden_panel = spread(hidden_rows, "z", Z).reshape(-1, quarter)
    piece_gate, piece_up = pieces[:, :half], pieces[:, half:]

    token_mine = rows_times(piece_gate, gate_mine) + rows_times(piece_up, up_mine)
    token_other = rows_times(piece_gate, gate_got) + rows_times(piece_up, up_got)
    token_mine, token_other = token_mine.astype(BF16), token_other.astype(BF16)
    token_part = jnp.where(
        core == 0,
        jnp.concatenate([token_mine, token_other], 1),
        jnp.concatenate([token_other, token_mine], 1),
    )
    output_part = times(hidden_panel, down_weight).astype(BF16)
    parts = jnp.concatenate([output_part, token_part], 1)
    parts = exchange(parts.reshape(CHIPS * CORES, mine_tokens, -1), ROW)
    output = total(parts[:, :, :width]).astype(BF16)
    terms = parts[:, :, width:].reshape(CHIPS, CORES, mine_tokens, features).astype(F32)
    terms = jnp.sum(terms, axis=1).astype(BF16).reshape(Z, 2, mine_tokens, features)
    terms = terms.transpose(0, 2, 1, 3).reshape(Z, mine_tokens, width)
    grad_tokens = total(exchange(terms, "z")).astype(BF16)

    grad_down_weight = columns_times(hidden_panel, cotangent).astype(BF16)

    def weight_grad(piece):
        mine = columns_times(panel_mine, piece).astype(BF16)
        other = columns_times(panel_other, piece).astype(BF16)
        got = lax.ppermute(other, "core", SWAP)
        return jnp.where(
            core == 0, jnp.concatenate([mine, got], 1), jnp.concatenate([got, mine], 1)
        )

    return output, grad_tokens, weight_grad(piece_gate), weight_grad(piece_up), grad_down_weight


def solution(mesh):
    fine = Mesh(mesh.devices.reshape(Y, X, CORES, Z), EVERY)
    spec = P(ROW, "z")
    return jax.shard_map(
        local, mesh=fine, in_specs=(spec,) * 5, out_specs=(spec,) * 5, check_vma=False
    )
```

```python
import jax
import jax.numpy as jnp
from jax import lax
from jax.experimental import pallas as pl
from jax.experimental.pallas import tpu as pltpu
from jax.sharding import Mesh, PartitionSpec as P

Y, X, CORES, Z = 4, 4, 2, 8
CHIPS = Y * X
ROWS = CHIPS * CORES
PLANE = ("y", "x")
ROW = ("y", "x", "core")
EVERY = ("y", "x", "core", "z")
SWAP = [(0, 1), (1, 0)]
BF16, F32 = jnp.bfloat16, jnp.float32
VMEM_LIMIT = 48 * 1024 * 1024


def rows_times(left, right):
    return lax.dot_general(left, right, (((1,), (1,)), ((), ())), preferred_element_type=F32)


def columns_times(left, right):
    return lax.dot_general(left, right, (((0,), (0,)), ((), ())), preferred_element_type=F32)


def times(left, right):
    return jnp.dot(left, right, preferred_element_type=F32)


def exchange(blocks, axis):
    return lax.all_to_all(blocks, axis, split_axis=0, concat_axis=0, tiled=True)


def total(blocks):
    return jnp.sum(blocks.astype(F32), axis=0)


def pairs(distance):
    return [(z, z ^ distance) for z in range(Z)]


def paired(at_core, own, got):
    return jnp.where(at_core == 0, jnp.stack([own, got]), jnp.stack([got, own]))


def gather_columns(block, late=()):
    z = lax.axis_index("z")
    share = block[None, None, None]
    for axis, distance in enumerate((4, 2, 1)):
        got = lax.ppermute(share, "z", pairs(distance))
        if axis == 0 and late:
            got, *late = lax.optimization_barrier((got, *late))
        low = (z // distance) % 2 == 0
        share = jnp.where(
            low, jnp.concatenate([share, got], axis), jnp.concatenate([got, share], axis)
        )
    share = share.reshape((Z,) + block.shape)
    return (share, *late) if late else share


def scatter_columns(blocks, after=None):
    z = lax.axis_index("z")
    share = blocks.reshape((2, 2, 2) + blocks.shape[1:])
    for axis, distance in ((2, 1), (1, 2), (0, 4)):
        bit = (z // distance) % 2
        keep = lax.dynamic_index_in_dim(share, bit, axis, keepdims=False)
        send = lax.dynamic_index_in_dim(share, 1 - bit, axis, keepdims=False)
        got = lax.ppermute(send, "z", pairs(distance))
        if axis == 2 and after is not None:
            got, after = lax.optimization_barrier((got, after))
        share = (keep.astype(F32) + got.astype(F32)).astype(BF16)
    return share if after is None else (share, after)


def owner_route():
    route = []
    for chip in range(CHIPS):
        for core in range(CORES):
            for z in range(Z):
                source = (chip * CORES + core) * Z + z
                target = ((2 * z + core) * CORES + chip % 2) * Z + chip // 2
                route.append((source, target))
    return route


TO_OWNER = owner_route()


def call(body, core, arrays, in_specs, out_shapes, out_specs, steps, scratch=(), aliases=None, cost=0):
    moved = sum(a.size * a.dtype.itemsize for a in arrays)
    return pl.pallas_call(
        body,
        grid_spec=pltpu.PrefetchScalarGridSpec(
            num_scalar_prefetch=1,
            grid=(steps,),
            in_specs=in_specs,
            out_specs=out_specs,
            scratch_shapes=list(scratch),
        ),
        out_shape=out_shapes,
        input_output_aliases=aliases or {},
        cost_estimate=pl.CostEstimate(flops=cost, bytes_accessed=moved, transcendentals=0),
        compiler_params=pltpu.CompilerParams(vmem_limit_bytes=VMEM_LIMIT),
    )(core, *arrays)


def my_columns(step, core, *_):
    return (0, 2 * core[0] + step)


def your_columns(step, core, *_):
    return (0, 2 * (1 - core[0]) + step)


def in_turn(step, *_):
    return (0, step)


def panels(core, panel_ref, depth):
    first, second = panel_ref[:, :depth], panel_ref[:, depth:]
    own = core[0] == 0
    return jnp.where(own, first, second), jnp.where(own, second, first)


def forward_products(core, arrivals, gate_weight, gate_got, up_weight, up_got):
    rows, depth = arrivals.shape[0], gate_weight.shape[0]
    quarter = gate_weight.shape[1] // 4

    def body(core, panel, gate_mine, gate_other, up_mine, up_other, out):
        mine, other = panels(core, panel, depth)
        gate = times(mine, gate_mine[...]) + times(other, gate_other[...])
        out[:, :quarter] = gate.astype(BF16)
        up = times(mine, up_mine[...]) + times(other, up_other[...])
        out[:, quarter:] = up.astype(BF16)

    weight = pl.BlockSpec((depth, quarter), my_columns)
    got = pl.BlockSpec((depth, quarter), in_turn)
    return call(
        body,
        core,
        (arrivals, gate_weight, gate_got, up_weight, up_got),
        [pl.BlockSpec((rows, 2 * depth), lambda step, core: (0, 0)), weight, got, weight, got],
        jax.ShapeDtypeStruct((rows, 4 * quarter), BF16),
        pl.BlockSpec((rows, 2 * quarter), in_turn),
        2,
        cost=16 * rows * depth * quarter,
    )


def activations(core, terms, grad_hidden):
    chips, tall, wide = terms.shape
    quarter = wide // 4

    def body(core, terms, grad_hidden, copies, keep, send):
        both = terms[0].astype(F32)
        for chip in range(1, chips):
            both = both + terms[chip].astype(F32)
        gate, up = both[:, :quarter], both[:, quarter:]
        sigmoid_gate = 1.0 / (1.0 + jnp.exp(-gate))
        silu_gate = gate * sigmoid_gate
        hidden = (silu_gate * up).astype(BF16)

        @pl.when(pl.program_id(0) == core[0])
        def _():
            keep[...] = hidden

        @pl.when(pl.program_id(0) != core[0])
        def _():
            send[...] = hidden

        cotangent = grad_hidden[0].astype(F32)
        grad_gate = cotangent * up * sigmoid_gate * (1.0 + gate * (1.0 - sigmoid_gate))
        grad_gate = grad_gate.astype(BF16)
        grad_up = (cotangent * silu_gate).astype(BF16)
        for chip in range(chips):
            copies[chip, :, :quarter] = grad_gate
            copies[chip, :, quarter:] = grad_up

    half = pl.BlockSpec((chips, tall, 2 * quarter), lambda step, core: (0, 0, step))
    flat = pl.BlockSpec((tall, quarter), lambda step, core: (0, 0))
    return call(
        body,
        core,
        (terms, grad_hidden),
        [half, pl.BlockSpec((1, tall, quarter), lambda step, core: (step, 0, 0))],
        [jax.ShapeDtypeStruct(terms.shape, BF16)]
        + [jax.ShapeDtypeStruct((tall, quarter), BF16)] * 2,
        [half, flat, flat],
        2,
        cost=30 * tall * wide,
    )


def token_products(core, pieces, gate_weight, gate_got, up_weight, up_got):
    depth = gate_weight.shape[0]
    rows, half = pieces.shape[0], pieces.shape[1] // 2
    quarter = half // 2

    def body(core, piece, gate_mine, gate_other, up_mine, up_other, out, mine, other):
        piece_gate, piece_up = piece[:, :quarter], piece[:, quarter:]
        term_mine = rows_times(piece_gate, gate_mine[...]) + rows_times(piece_up, up_mine[...])
        term_other = rows_times(piece_gate, gate_other[...]) + rows_times(piece_up, up_other[...])

        @pl.when(pl.program_id(0) == 0)
        def _():
            mine[...] = term_mine
            other[...] = term_other

        @pl.when(pl.program_id(0) == 1)
        def _():
            sum_mine = (mine[...] + term_mine).astype(BF16)
            sum_other = (other[...] + term_other).astype(BF16)
            own = core[0] == 0
            out[:, :depth] = jnp.where(own, sum_mine, sum_other)
            out[:, depth:] = jnp.where(own, sum_other, sum_mine)

    weight = pl.BlockSpec((depth, quarter), my_columns)
    got = pl.BlockSpec((depth, quarter), in_turn)
    return call(
        body,
        core,
        (pieces, gate_weight, gate_got, up_weight, up_got),
        [
            pl.BlockSpec((rows, half), in_turn),
            weight,
            got,
            weight,
            got,
        ],
        jax.ShapeDtypeStruct((rows, 2 * depth), BF16),
        pl.BlockSpec((rows, 2 * depth), lambda step, core: (0, 0)),
        2,
        scratch=[pltpu.VMEM((rows, depth), F32)] * 2,
        cost=16 * rows * depth * quarter,
    )


def output_product(core, hidden_panel, down_weight, token_part):
    rows, quarter = hidden_panel.shape
    width, features = down_weight.shape[1], token_part.shape[1]

    def body(core, hidden, down, tokens, out):
        out[:, :width] = times(hidden[...], down[...]).astype(BF16)
        out[:, width:] = tokens[...]

    def whole(*shape):
        return pl.BlockSpec(shape, lambda step, core: (0, 0))

    return call(
        body,
        core,
        (hidden_panel, down_weight, token_part),
        [whole(rows, quarter), whole(quarter, width), whole(rows, features)],
        jax.ShapeDtypeStruct((rows, width + features), BF16),
        whole(rows, width + features),
        1,
        cost=2 * rows * quarter * width,
    )


def weight_grads(core, arrivals, pieces, depth):
    rows = arrivals.shape[0]
    wide = pieces.shape[1] // 2
    quarter = wide // 2

    def body(core, panel, piece, gate_grad, up_grad, gate_send, up_send):
        mine, other = panels(core, panel, depth)
        piece_gate, piece_up = piece[:, :quarter], piece[:, quarter:]
        gate_send[...] = columns_times(other, piece_gate).astype(BF16)
        up_send[...] = columns_times(other, piece_up).astype(BF16)
        gate_grad[...] = columns_times(mine, piece_gate).astype(BF16)
        up_grad[...] = columns_times(mine, piece_up).astype(BF16)

    mine = pl.BlockSpec((depth, quarter), my_columns)
    send = pl.BlockSpec((depth, quarter), in_turn)
    return call(
        body,
        core,
        (arrivals, pieces),
        [
            pl.BlockSpec((rows, 2 * depth), lambda step, core: (0, 0)),
            pl.BlockSpec((rows, wide), in_turn),
        ],
        [jax.ShapeDtypeStruct((depth, 4 * quarter), BF16)] * 2
        + [jax.ShapeDtypeStruct((depth, 2 * quarter), BF16)] * 2,
        [mine, mine, send, send],
        2,
        cost=16 * rows * depth * quarter,
    )


def fill(core, gate_grad, up_grad, gate_got, up_got):
    depth, units = gate_grad.shape
    quarter = units // 4

    def body(core, _, __, gate_got, up_got, gate_out, up_out):
        gate_out[...] = gate_got[...]
        up_out[...] = up_got[...]

    anywhere = pl.BlockSpec(memory_space=pl.ANY)
    got = pl.BlockSpec((depth, quarter), in_turn)
    out = pl.BlockSpec((depth, quarter), your_columns)
    return call(
        body,
        core,
        (gate_grad, up_grad, gate_got, up_got),
        [anywhere, anywhere, got, got],
        [jax.ShapeDtypeStruct(gate_grad.shape, BF16)] * 2,
        [out, out],
        2,
        aliases={1: 0, 2: 1},
    )


def local(tokens, gate_weight, up_weight, down_weight, out_grad):
    at_core = lax.axis_index("core")
    core = at_core.astype(jnp.int32).reshape(1)
    few, width = tokens.shape
    depth, units = gate_weight.shape
    half, quarter = units // 2, units // 4

    def swapped_half(weight):
        theirs = lax.dynamic_slice_in_dim(weight, (1 - at_core) * half, half, 1)
        return lax.ppermute(theirs, "core", SWAP)

    features = 2 * depth
    copies = jnp.broadcast_to(out_grad[None], (ROWS, few, width))
    cotangent = exchange(copies, ROW).reshape(ROWS * few, width)

    parts, gate_late, up_late = gather_columns(tokens, (gate_weight, up_weight))
    parts = parts.reshape(Z, few, 2, features).transpose(0, 2, 1, 3)
    parts = parts.reshape(CHIPS, 1, few, features)
    parts = jnp.broadcast_to(parts, (CHIPS, CORES, few, features))
    parts = parts.reshape(ROWS, few, features)
    parts, cotangent = lax.optimization_barrier((parts, cotangent))
    arrivals = exchange(parts, ROW).reshape(ROWS * few, features)

    hidden_part = rows_times(cotangent, down_weight).astype(BF16)
    hidden_sum, arrivals = scatter_columns(hidden_part.reshape(Z, -1, quarter), arrivals)
    hidden_sum = hidden_sum.reshape(2, -1, quarter)
    hidden_keep = lax.dynamic_index_in_dim(hidden_sum, at_core, 0, keepdims=False)
    hidden_send = lax.dynamic_index_in_dim(hidden_sum, 1 - at_core, 0, keepdims=False)
    hidden_sum = paired(at_core, hidden_keep, lax.ppermute(hidden_send, "core", SWAP))
    grad_hidden = lax.ppermute(hidden_sum, EVERY, TO_OWNER)

    gate_got, up_got = swapped_half(gate_late), swapped_half(up_late)
    sent = forward_products(core, arrivals, gate_weight, gate_got, up_weight, up_got)

    terms = exchange(sent.reshape(CHIPS, -1, units), PLANE)
    copies, hidden_keep, hidden_send = activations(core, terms, grad_hidden)
    hidden = paired(at_core, hidden_keep, lax.ppermute(hidden_send, "core", SWAP))
    hidden = gather_columns(hidden).reshape(CHIPS, -1, quarter)
    pieces = exchange(copies, PLANE).reshape(-1, units)
    pieces, hidden = lax.optimization_barrier((pieces, hidden))
    hidden_panel = exchange(hidden, PLANE).reshape(-1, quarter)

    token_part = token_products(core, pieces, gate_weight, gate_got, up_weight, up_got)
    parts = output_product(core, hidden_panel, down_weight, token_part)
    parts = exchange(parts.reshape(ROWS, few, width + features), ROW)

    gate_grad, up_grad, gate_send, up_send = weight_grads(core, arrivals, pieces, depth)
    grad_down_weight = columns_times(hidden_panel, cotangent).astype(BF16)
    parts, gate_send, grad_down_weight = lax.optimization_barrier(
        (parts, gate_send, grad_down_weight)
    )
    output = total(parts[:, :, :width]).astype(BF16)
    terms = parts[:, :, width:].reshape(CHIPS, CORES, few, features).astype(F32)
    terms = jnp.sum(terms, axis=1).astype(BF16).reshape(Z, 2, few, features)
    terms = terms.transpose(0, 2, 1, 3).reshape(Z, few, width)
    terms = exchange(terms, "z")

    gate_back = lax.ppermute(gate_send, "core", SWAP)
    up_back = lax.ppermute(up_send, "core", SWAP)
    gate_grad, up_grad = fill(core, gate_grad, up_grad, gate_back, up_back)
    terms, gate_grad, up_grad = lax.optimization_barrier((terms, gate_grad, up_grad))
    grad_tokens = total(terms).astype(BF16)
    return output, grad_tokens, gate_grad, up_grad, grad_down_weight


def solution(mesh):
    fine = Mesh(mesh.devices.reshape(Y, X, CORES, Z), EVERY)
    spec = P(ROW, "z")
    return jax.shard_map(
        local, mesh=fine, in_specs=(spec,) * 5, out_specs=(spec,) * 5, check_vma=False
    )
```

```python
import jax
import jax.numpy as jnp
from jax import lax
from jax.experimental import pallas as pl
from jax.experimental.pallas import tpu as pltpu
from jax.sharding import Mesh, PartitionSpec as P

Y, X, CORES, Z = 4, 4, 2, 8
CHIPS = Y * X
ROWS = CHIPS * CORES
PLANE = ("y", "x")
ROW = ("y", "x", "core")
EVERY = ("y", "x", "core", "z")
SWAP = [(0, 1), (1, 0)]
BF16, F32 = jnp.bfloat16, jnp.float32
VMEM_LIMIT = 48 * 1024 * 1024


def rows_times(left, right):
    return lax.dot_general(left, right, (((1,), (1,)), ((), ())), preferred_element_type=F32)


def columns_times(left, right):
    return lax.dot_general(left, right, (((0,), (0,)), ((), ())), preferred_element_type=F32)


def times(left, right):
    return jnp.dot(left, right, preferred_element_type=F32)


def exchange(blocks, axis):
    return lax.all_to_all(blocks, axis, split_axis=0, concat_axis=0, tiled=True)


def total(blocks):
    return jnp.sum(blocks.astype(F32), axis=0)


def pairs(distance):
    return [(z, z ^ distance) for z in range(Z)]


def paired(at_core, own, got):
    return jnp.where(at_core == 0, jnp.stack([own, got]), jnp.stack([got, own]))


def gather_columns(block, late=()):
    z = lax.axis_index("z")
    share = block[None, None, None]
    for axis, distance in enumerate((4, 2, 1)):
        got = lax.ppermute(share, "z", pairs(distance))
        if axis == 0 and late:
            got, *late = lax.optimization_barrier((got, *late))
        low = (z // distance) % 2 == 0
        share = jnp.where(
            low, jnp.concatenate([share, got], axis), jnp.concatenate([got, share], axis)
        )
    share = share.reshape((Z,) + block.shape)
    return (share, *late) if late else share


def near_order(z, near):
    near = [jnp.where(z % 2 == 0, near[at], near[at ^ 1]) for at in range(4)]
    return [jnp.where(z // 2 % 2 == 0, near[at], near[at ^ 2]) for at in range(4)]


def gather_hidden(block):
    z = lax.axis_index("z")
    got = lax.ppermute(block, "z", pairs(4))
    low = z < 4
    share = jnp.where(low, jnp.stack([block, got]), jnp.stack([got, block]))
    near = [share] + [lax.ppermute(share, "z", pairs(distance)) for distance in (1, 2, 3)]
    return jnp.stack(near_order(z, near), 1).reshape((Z,) + block.shape)


def near_exchange(blocks):
    z = lax.axis_index("z")
    share = blocks.reshape((2, 4) + blocks.shape[1:])
    near = [
        lax.dynamic_index_in_dim(share, (z % 4) ^ distance, 1, keepdims=False)
        for distance in range(4)
    ]
    return near[0], [lax.ppermute(near[d], "z", pairs(d)) for d in (1, 2, 3)]


def far_exchange(own, got):
    z = lax.axis_index("z")
    share = own.astype(F32)
    for term in got:
        share = share + term.astype(F32)
    share = share.astype(BF16)
    keep = lax.dynamic_index_in_dim(share, z // 4, 0, keepdims=False)
    send = lax.dynamic_index_in_dim(share, 1 - z // 4, 0, keepdims=False)
    far = lax.ppermute(send, "z", pairs(4))
    return (keep.astype(F32) + far.astype(F32)).astype(BF16)


def owner_route():
    route = []
    for chip in range(CHIPS):
        for core in range(CORES):
            for z in range(Z):
                source = (chip * CORES + core) * Z + z
                target = ((2 * z + core) * CORES + chip % 2) * Z + chip // 2
                route.append((source, target))
    return route


TO_OWNER = owner_route()


def in_hbm(array):
    return pltpu.with_memory_space_constraint(array, pltpu.HBM)


def call(body, core, arrays, in_specs, out_shapes, out_specs, steps, scratch=(), aliases=None, cost=0):
    moved = sum(a.size * a.dtype.itemsize for a in arrays)
    return pl.pallas_call(
        body,
        grid_spec=pltpu.PrefetchScalarGridSpec(
            num_scalar_prefetch=1,
            grid=(steps,),
            in_specs=in_specs,
            out_specs=out_specs,
            scratch_shapes=list(scratch),
        ),
        out_shape=out_shapes,
        input_output_aliases=aliases or {},
        cost_estimate=pl.CostEstimate(flops=cost, bytes_accessed=moved, transcendentals=0),
        compiler_params=pltpu.CompilerParams(vmem_limit_bytes=VMEM_LIMIT),
    )(core, *arrays)


def my_columns(step, core, *_):
    return (0, 2 * core[0] + step)


def your_columns(step, core, *_):
    return (0, 2 * (1 - core[0]) + step)


def in_turn(step, *_):
    return (0, step)


def panels(core, panel_ref, depth):
    first, second = panel_ref[:, :depth], panel_ref[:, depth:]
    own = core[0] == 0
    return jnp.where(own, first, second), jnp.where(own, second, first)


def forward_products(core, arrivals, gate_weight, gate_got, up_weight, up_got):
    rows, depth = arrivals.shape[0], gate_weight.shape[0]
    quarter = gate_weight.shape[1] // 4

    def body(core, panel, gate_mine, gate_other, up_mine, up_other, out):
        mine, other = panels(core, panel, depth)
        gate = times(mine, gate_mine[...]) + times(other, gate_other[...])
        out[:, :quarter] = gate.astype(BF16)
        up = times(mine, up_mine[...]) + times(other, up_other[...])
        out[:, quarter:] = up.astype(BF16)

    weight = pl.BlockSpec((depth, quarter), my_columns)
    got = pl.BlockSpec((depth, quarter), in_turn)
    return call(
        body,
        core,
        (arrivals, in_hbm(gate_weight), gate_got, in_hbm(up_weight), up_got),
        [pl.BlockSpec((rows, 2 * depth), lambda step, core: (0, 0)), weight, got, weight, got],
        pltpu.HBM((rows, 4 * quarter), BF16),
        pl.BlockSpec((rows, 2 * quarter), in_turn),
        2,
        cost=16 * rows * depth * quarter,
    )


def activations(core, terms, grad_hidden):
    chips, tall, wide = terms.shape
    quarter = wide // 4

    def body(core, terms, grad_hidden, copies, keep, send):
        both = terms[0].astype(F32)
        for chip in range(1, chips):
            both = both + terms[chip].astype(F32)
        gate, up = both[:, :quarter], both[:, quarter:]
        sigmoid_gate = 1.0 / (1.0 + jnp.exp(-gate))
        silu_gate = gate * sigmoid_gate
        hidden = (silu_gate * up).astype(BF16)

        @pl.when(pl.program_id(0) == core[0])
        def _():
            keep[...] = hidden

        @pl.when(pl.program_id(0) != core[0])
        def _():
            send[...] = hidden

        cotangent = grad_hidden[0].astype(F32)
        grad_gate = cotangent * up * sigmoid_gate * (1.0 + gate * (1.0 - sigmoid_gate))
        grad_gate = grad_gate.astype(BF16)
        grad_up = (cotangent * silu_gate).astype(BF16)
        for chip in range(chips):
            copies[chip, :, :quarter] = grad_gate
            copies[chip, :, quarter:] = grad_up

    half = pl.BlockSpec((chips, tall, 2 * quarter), lambda step, core: (0, 0, step))
    flat = pl.BlockSpec((tall, quarter), lambda step, core: (0, 0))
    return call(
        body,
        core,
        (terms, grad_hidden),
        [half, pl.BlockSpec((1, tall, quarter), lambda step, core: (step, 0, 0))],
        [pltpu.HBM(terms.shape, BF16)]
        + [jax.ShapeDtypeStruct((tall, quarter), BF16)] * 2,
        [half, flat, flat],
        2,
        cost=30 * tall * wide,
    )


def token_products(core, pieces, gate_weight, gate_got, up_weight, up_got):
    depth = gate_weight.shape[0]
    rows, half = pieces.shape[0], pieces.shape[1] // 2
    quarter = half // 2

    def body(core, piece, gate_mine, gate_other, up_mine, up_other, out, mine, other):
        piece_gate, piece_up = piece[:, :quarter], piece[:, quarter:]
        term_mine = rows_times(piece_gate, gate_mine[...]) + rows_times(piece_up, up_mine[...])
        term_other = rows_times(piece_gate, gate_other[...]) + rows_times(piece_up, up_other[...])

        @pl.when(pl.program_id(0) == 0)
        def _():
            mine[...] = term_mine
            other[...] = term_other

        @pl.when(pl.program_id(0) == 1)
        def _():
            sum_mine = (mine[...] + term_mine).astype(BF16)
            sum_other = (other[...] + term_other).astype(BF16)
            own = core[0] == 0
            out[:, :depth] = jnp.where(own, sum_mine, sum_other)
            out[:, depth:] = jnp.where(own, sum_other, sum_mine)

    weight = pl.BlockSpec((depth, quarter), my_columns)
    got = pl.BlockSpec((depth, quarter), in_turn)
    return call(
        body,
        core,
        (pieces, in_hbm(gate_weight), gate_got, in_hbm(up_weight), up_got),
        [
            pl.BlockSpec((rows, half), in_turn),
            weight,
            got,
            weight,
            got,
        ],
        jax.ShapeDtypeStruct((rows, 2 * depth), BF16),
        pl.BlockSpec((rows, 2 * depth), lambda step, core: (0, 0)),
        2,
        scratch=[pltpu.VMEM((rows, depth), F32)] * 2,
        cost=16 * rows * depth * quarter,
    )


def weight_grads(core, arrivals, pieces, depth):
    rows = arrivals.shape[0]
    wide = pieces.shape[1] // 2
    quarter = wide // 2

    def body(core, panel, piece, gate_grad, up_grad, gate_send, up_send):
        mine, other = panels(core, panel, depth)
        piece_gate, piece_up = piece[:, :quarter], piece[:, quarter:]
        gate_send[...] = columns_times(other, piece_gate).astype(BF16)
        up_send[...] = columns_times(other, piece_up).astype(BF16)
        gate_grad[...] = columns_times(mine, piece_gate).astype(BF16)
        up_grad[...] = columns_times(mine, piece_up).astype(BF16)

    mine = pl.BlockSpec((depth, quarter), my_columns)
    send = pl.BlockSpec((depth, quarter), in_turn)
    return call(
        body,
        core,
        (arrivals, pieces),
        [
            pl.BlockSpec((rows, 2 * depth), lambda step, core: (0, 0)),
            pl.BlockSpec((rows, wide), in_turn),
        ],
        [jax.ShapeDtypeStruct((depth, 4 * quarter), BF16)] * 2
        + [jax.ShapeDtypeStruct((depth, 2 * quarter), BF16)] * 2,
        [mine, mine, send, send],
        2,
        cost=16 * rows * depth * quarter,
    )


def fill(core, gate_grad, up_grad, gate_got, up_got):
    depth, units = gate_grad.shape
    quarter = units // 4

    def body(core, _, __, gate_got, up_got, gate_out, up_out):
        gate_out[...] = gate_got[...]
        up_out[...] = up_got[...]

    anywhere = pl.BlockSpec(memory_space=pl.ANY)
    got = pl.BlockSpec((depth, quarter), in_turn)
    out = pl.BlockSpec((depth, quarter), your_columns)
    return call(
        body,
        core,
        (gate_grad, up_grad, gate_got, up_got),
        [anywhere, anywhere, got, got],
        [jax.ShapeDtypeStruct(gate_grad.shape, BF16)] * 2,
        [out, out],
        2,
        aliases={1: 0, 2: 1},
    )


def local(tokens, gate_weight, up_weight, down_weight, out_grad):
    at_core = lax.axis_index("core")
    core = at_core.astype(jnp.int32).reshape(1)
    few, width = tokens.shape
    depth, units = gate_weight.shape
    half, quarter = units // 2, units // 4

    def swapped_half(weight):
        theirs = lax.dynamic_slice_in_dim(weight, (1 - at_core) * half, half, 1)
        return lax.ppermute(theirs, "core", SWAP)

    features = 2 * depth
    copies = jnp.broadcast_to(out_grad[None], (ROWS, few, width))
    cotangent = exchange(copies, ROW).reshape(ROWS * few, width)

    parts, gate_late, up_late = gather_columns(tokens, (gate_weight, up_weight))
    parts = parts.reshape(Z, few, 2, features).transpose(0, 2, 1, 3)
    parts = parts.reshape(CHIPS, 1, few, features)
    parts = jnp.broadcast_to(parts, (CHIPS, CORES, few, features))
    parts = parts.reshape(ROWS, few, features)
    parts, cotangent = lax.optimization_barrier((parts, cotangent))
    arrivals = exchange(parts, ROW).reshape(ROWS * few, features)

    hidden_part = rows_times(cotangent, down_weight).astype(BF16)
    gate_got, up_got = swapped_half(gate_late), swapped_half(up_late)
    own, got = near_exchange(hidden_part.reshape(Z, -1, quarter))
    got[0], arrivals = lax.optimization_barrier((got[0], arrivals))
    sent = forward_products(core, arrivals, gate_weight, gate_got, up_weight, up_got)
    got[1], sent = lax.optimization_barrier((got[1], sent))
    hidden_sum = far_exchange(own, got)
    hidden_sum = hidden_sum.reshape(2, -1, quarter)
    hidden_keep = lax.dynamic_index_in_dim(hidden_sum, at_core, 0, keepdims=False)
    hidden_send = lax.dynamic_index_in_dim(hidden_sum, 1 - at_core, 0, keepdims=False)
    hidden_sum = paired(at_core, hidden_keep, lax.ppermute(hidden_send, "core", SWAP))
    grad_hidden = lax.ppermute(hidden_sum, EVERY, TO_OWNER)

    terms = exchange(sent.reshape(CHIPS, -1, units), PLANE)
    copies, hidden_keep, hidden_send = activations(core, terms, grad_hidden)
    hidden = paired(at_core, hidden_keep, lax.ppermute(hidden_send, "core", SWAP))
    hidden = gather_hidden(hidden).reshape(CHIPS, -1, quarter)
    pieces = exchange(copies, PLANE).reshape(-1, units)
    parts = token_products(core, pieces, gate_weight, gate_got, up_weight, up_got)
    parts = exchange(parts.reshape(ROWS, few, features), ROW)
    gate_grad, up_grad, gate_send, up_send = weight_grads(core, arrivals, pieces, depth)
    parts, hidden, gate_send = lax.optimization_barrier((parts, hidden, gate_send))
    hidden_panel = exchange(hidden, PLANE).reshape(-1, quarter)

    terms = parts.reshape(CHIPS, CORES, few, features).astype(F32)
    terms = jnp.sum(terms, axis=1).astype(BF16).reshape(Z, 2, few, features)
    terms = terms.transpose(0, 2, 1, 3).reshape(Z, few, width)
    own, got = near_exchange(terms)

    output = times(hidden_panel, down_weight).astype(BF16).reshape(ROWS, few, width)
    output = exchange(output, ROW)
    grad_tokens = far_exchange(own, got)

    gate_back = lax.ppermute(gate_send, "core", SWAP)
    up_back = lax.ppermute(up_send, "core", SWAP)
    gate_grad, up_grad = fill(core, gate_grad, up_grad, gate_back, up_back)
    grad_down_weight = columns_times(hidden_panel, cotangent).astype(BF16)
    output, grad_tokens, gate_grad, up_grad, grad_down_weight = lax.optimization_barrier(
        (output, grad_tokens, gate_grad, up_grad, grad_down_weight)
    )
    output = total(output).astype(BF16)
    return output, grad_tokens, gate_grad, up_grad, grad_down_weight


def solution(mesh):
    fine = Mesh(mesh.devices.reshape(Y, X, CORES, Z), EVERY)
    spec = P(ROW, "z")
    return jax.shard_map(
        local, mesh=fine, in_specs=(spec,) * 5, out_specs=(spec,) * 5, check_vma=False
    )
```

```python
import jax
import jax.numpy as jnp
from jax import lax
from jax.experimental import pallas as pl
from jax.experimental.pallas import tpu as pltpu
from jax.sharding import Mesh, PartitionSpec as P

Y, X, CORES, Z = 4, 4, 2, 8
CHIPS = Y * X
ROWS = CHIPS * CORES
PLANE = ("y", "x")
ROW = ("y", "x", "core")
EVERY = ("y", "x", "core", "z")
SWAP = [(0, 1), (1, 0)]
BF16, F32 = jnp.bfloat16, jnp.float32
VMEM_LIMIT = 48 * 1024 * 1024


def rows_times(left, right):
    return lax.dot_general(left, right, (((1,), (1,)), ((), ())), preferred_element_type=F32)


def columns_times(left, right):
    return lax.dot_general(left, right, (((0,), (0,)), ((), ())), preferred_element_type=F32)


def times(left, right):
    return jnp.dot(left, right, preferred_element_type=F32)


def exchange(blocks, axis):
    return lax.all_to_all(blocks, axis, split_axis=0, concat_axis=0, tiled=True)


def total(blocks):
    return jnp.sum(blocks.astype(F32), axis=0)


def pairs(distance):
    return [(z, z ^ distance) for z in range(Z)]


def paired(at_core, own, got):
    return jnp.where(at_core == 0, jnp.stack([own, got]), jnp.stack([got, own]))


def gather_columns(block, late=()):
    z = lax.axis_index("z")
    share = block[None, None, None]
    for axis, distance in enumerate((4, 2, 1)):
        got = lax.ppermute(share, "z", pairs(distance))
        if axis == 0 and late:
            got, *late = lax.optimization_barrier((got, *late))
        low = (z // distance) % 2 == 0
        share = jnp.where(
            low, jnp.concatenate([share, got], axis), jnp.concatenate([got, share], axis)
        )
    share = share.reshape((Z,) + block.shape)
    return (share, *late) if late else share


def near_order(z, near):
    near = [jnp.where(z % 2 == 0, near[at], near[at ^ 1]) for at in range(4)]
    return [jnp.where(z // 2 % 2 == 0, near[at], near[at ^ 2]) for at in range(4)]


def gather_hidden(block):
    z = lax.axis_index("z")
    got = lax.ppermute(block, "z", pairs(4))
    low = z < 4
    share = jnp.where(low, jnp.stack([block, got]), jnp.stack([got, block]))
    near = [share] + [lax.ppermute(share, "z", pairs(distance)) for distance in (1, 2, 3)]
    return jnp.stack(near_order(z, near), 1).reshape((Z,) + block.shape)


def near_exchange(blocks):
    z = lax.axis_index("z")
    share = blocks.reshape((2, 4) + blocks.shape[1:])
    near = [
        lax.dynamic_index_in_dim(share, (z % 4) ^ distance, 1, keepdims=False)
        for distance in range(4)
    ]
    return near[0], [lax.ppermute(near[d], "z", pairs(d)) for d in (1, 2, 3)]


def far_exchange(own, got):
    z = lax.axis_index("z")
    share = own.astype(F32)
    for term in got:
        share = share + term.astype(F32)
    share = share.astype(BF16)
    keep = lax.dynamic_index_in_dim(share, z // 4, 0, keepdims=False)
    send = lax.dynamic_index_in_dim(share, 1 - z // 4, 0, keepdims=False)
    far = lax.ppermute(send, "z", pairs(4))
    return (keep.astype(F32) + far.astype(F32)).astype(BF16)


def owner_route():
    route = []
    for chip in range(CHIPS):
        for core in range(CORES):
            for z in range(Z):
                source = (chip * CORES + core) * Z + z
                target = ((2 * z + core) * CORES + chip % 2) * Z + chip // 2
                route.append((source, target))
    return route


TO_OWNER = owner_route()


def in_hbm(array):
    return pltpu.with_memory_space_constraint(array, pltpu.HBM)


def call(body, core, arrays, in_specs, out_shapes, out_specs, steps, scratch=(), aliases=None, cost=0):
    moved = sum(a.size * a.dtype.itemsize for a in arrays)
    return pl.pallas_call(
        body,
        grid_spec=pltpu.PrefetchScalarGridSpec(
            num_scalar_prefetch=1,
            grid=(steps,),
            in_specs=in_specs,
            out_specs=out_specs,
            scratch_shapes=list(scratch),
        ),
        out_shape=out_shapes,
        input_output_aliases=aliases or {},
        cost_estimate=pl.CostEstimate(flops=cost, bytes_accessed=moved, transcendentals=0),
        compiler_params=pltpu.CompilerParams(vmem_limit_bytes=VMEM_LIMIT),
    )(core, *arrays)


def my_columns(step, core, *_):
    return (0, 2 * core[0] + step)


def your_columns(step, core, *_):
    return (0, 2 * (1 - core[0]) + step)


def in_turn(step, *_):
    return (0, step)


def panels(core, panel_ref, depth):
    first, second = panel_ref[:, :depth], panel_ref[:, depth:]
    own = core[0] == 0
    return jnp.where(own, first, second), jnp.where(own, second, first)


def forward_products(core, arrivals, gate_weight, gate_got, up_weight, up_got):
    rows, depth = arrivals.shape[0], gate_weight.shape[0]
    quarter = gate_weight.shape[1] // 4

    def body(core, panel, gate_mine, gate_other, up_mine, up_other, out):
        mine, other = panels(core, panel, depth)
        gate = times(mine, gate_mine[...]) + times(other, gate_other[...])
        out[:, :quarter] = gate.astype(BF16)
        up = times(mine, up_mine[...]) + times(other, up_other[...])
        out[:, quarter:] = up.astype(BF16)

    weight = pl.BlockSpec((depth, quarter), my_columns)
    got = pl.BlockSpec((depth, quarter), in_turn)
    return call(
        body,
        core,
        (arrivals, in_hbm(gate_weight), gate_got, in_hbm(up_weight), up_got),
        [pl.BlockSpec((rows, 2 * depth), lambda step, core: (0, 0)), weight, got, weight, got],
        pltpu.HBM((rows, 4 * quarter), BF16),
        pl.BlockSpec((rows, 2 * quarter), in_turn),
        2,
        cost=16 * rows * depth * quarter,
    )


def activations(core, terms):
    chips, tall, wide = terms.shape
    quarter = wide // 4

    def body(core, terms, factors, keep, send):
        both = terms[0].astype(F32)
        for chip in range(1, chips):
            both = both + terms[chip].astype(F32)
        gate, up = both[:, :quarter], both[:, quarter:]
        sigmoid_gate = 1.0 / (1.0 + jnp.exp(-gate))
        silu_gate = gate * sigmoid_gate
        factors[:, :quarter] = up * sigmoid_gate * (1.0 + gate * (1.0 - sigmoid_gate))
        factors[:, quarter:] = silu_gate
        hidden = (silu_gate * up).astype(BF16)

        @pl.when(pl.program_id(0) == core[0])
        def _():
            keep[...] = hidden

        @pl.when(pl.program_id(0) != core[0])
        def _():
            send[...] = hidden

    half = pl.BlockSpec((chips, tall, 2 * quarter), lambda step, core: (0, 0, step))
    flat = pl.BlockSpec((tall, quarter), lambda step, core: (0, 0))
    return call(
        body,
        core,
        (terms,),
        [half],
        [jax.ShapeDtypeStruct((tall, wide), F32)]
        + [jax.ShapeDtypeStruct((tall, quarter), BF16)] * 2,
        [pl.BlockSpec((tall, 2 * quarter), in_turn), flat, flat],
        2,
        cost=30 * tall * wide,
    )


def unit_grads(core, factors, grad_hidden, chips):
    tall, wide = factors.shape
    quarter = wide // 4

    def body(core, factors, grad_hidden, copies):
        cotangent = grad_hidden[0].astype(F32)
        grad_gate = (cotangent * factors[:, :quarter]).astype(BF16)
        grad_up = (cotangent * factors[:, quarter:]).astype(BF16)
        for chip in range(chips):
            copies[chip, :, :quarter] = grad_gate
            copies[chip, :, quarter:] = grad_up

    return call(
        body,
        core,
        (factors, grad_hidden),
        [
            pl.BlockSpec((tall, 2 * quarter), in_turn),
            pl.BlockSpec((1, tall, quarter), lambda step, core: (step, 0, 0)),
        ],
        pltpu.HBM((chips, tall, wide), BF16),
        pl.BlockSpec((chips, tall, 2 * quarter), lambda step, core: (0, 0, step)),
        2,
        cost=2 * tall * wide,
    )


def token_products(core, pieces, gate_weight, gate_got, up_weight, up_got):
    depth = gate_weight.shape[0]
    rows, half = pieces.shape[0], pieces.shape[1] // 2
    quarter = half // 2

    def body(core, piece, gate_mine, gate_other, up_mine, up_other, out, mine, other):
        piece_gate, piece_up = piece[:, :quarter], piece[:, quarter:]
        term_mine = rows_times(piece_gate, gate_mine[...]) + rows_times(piece_up, up_mine[...])
        term_other = rows_times(piece_gate, gate_other[...]) + rows_times(piece_up, up_other[...])

        @pl.when(pl.program_id(0) == 0)
        def _():
            mine[...] = term_mine
            other[...] = term_other

        @pl.when(pl.program_id(0) == 1)
        def _():
            sum_mine = (mine[...] + term_mine).astype(BF16)
            sum_other = (other[...] + term_other).astype(BF16)
            own = core[0] == 0
            out[:, :depth] = jnp.where(own, sum_mine, sum_other)
            out[:, depth:] = jnp.where(own, sum_other, sum_mine)

    weight = pl.BlockSpec((depth, quarter), my_columns)
    got = pl.BlockSpec((depth, quarter), in_turn)
    return call(
        body,
        core,
        (pieces, in_hbm(gate_weight), gate_got, in_hbm(up_weight), up_got),
        [
            pl.BlockSpec((rows, half), in_turn),
            weight,
            got,
            weight,
            got,
        ],
        jax.ShapeDtypeStruct((rows, 2 * depth), BF16),
        pl.BlockSpec((rows, 2 * depth), lambda step, core: (0, 0)),
        2,
        scratch=[pltpu.VMEM((rows, depth), F32)] * 2,
        cost=16 * rows * depth * quarter,
    )


def weight_grads(core, arrivals, pieces, depth):
    rows = arrivals.shape[0]
    wide = pieces.shape[1] // 2
    quarter = wide // 2

    def body(core, panel, piece, gate_grad, up_grad, gate_send, up_send):
        mine, other = panels(core, panel, depth)
        piece_gate, piece_up = piece[:, :quarter], piece[:, quarter:]
        gate_send[...] = columns_times(other, piece_gate).astype(BF16)
        up_send[...] = columns_times(other, piece_up).astype(BF16)
        gate_grad[...] = columns_times(mine, piece_gate).astype(BF16)
        up_grad[...] = columns_times(mine, piece_up).astype(BF16)

    mine = pl.BlockSpec((depth, quarter), my_columns)
    send = pl.BlockSpec((depth, quarter), in_turn)
    return call(
        body,
        core,
        (arrivals, pieces),
        [
            pl.BlockSpec((rows, 2 * depth), lambda step, core: (0, 0)),
            pl.BlockSpec((rows, wide), in_turn),
        ],
        [jax.ShapeDtypeStruct((depth, 4 * quarter), BF16)] * 2
        + [jax.ShapeDtypeStruct((depth, 2 * quarter), BF16)] * 2,
        [mine, mine, send, send],
        2,
        cost=16 * rows * depth * quarter,
    )


def fill(core, gate_grad, up_grad, gate_got, up_got):
    depth, units = gate_grad.shape
    quarter = units // 4

    def body(core, _, __, gate_got, up_got, gate_out, up_out):
        gate_out[...] = gate_got[...]
        up_out[...] = up_got[...]

    anywhere = pl.BlockSpec(memory_space=pl.ANY)
    got = pl.BlockSpec((depth, quarter), in_turn)
    out = pl.BlockSpec((depth, quarter), your_columns)
    return call(
        body,
        core,
        (gate_grad, up_grad, gate_got, up_got),
        [anywhere, anywhere, got, got],
        [jax.ShapeDtypeStruct(gate_grad.shape, BF16)] * 2,
        [out, out],
        2,
        aliases={1: 0, 2: 1},
    )


def local(tokens, gate_weight, up_weight, down_weight, out_grad):
    at_core = lax.axis_index("core")
    core = at_core.astype(jnp.int32).reshape(1)
    few, width = tokens.shape
    depth, units = gate_weight.shape
    half, quarter = units // 2, units // 4

    def swapped_half(weight):
        theirs = lax.dynamic_slice_in_dim(weight, (1 - at_core) * half, half, 1)
        return lax.ppermute(theirs, "core", SWAP)

    features = 2 * depth
    copies = jnp.broadcast_to(out_grad[None], (ROWS, few, width))
    cotangent = exchange(copies, ROW).reshape(ROWS * few, width)

    parts, gate_late, up_late = gather_columns(tokens, (gate_weight, up_weight))
    parts = parts.reshape(Z, few, 2, features).transpose(0, 2, 1, 3)
    parts = parts.reshape(CHIPS, 1, few, features)
    parts = jnp.broadcast_to(parts, (CHIPS, CORES, few, features))
    parts = parts.reshape(ROWS, few, features)
    parts, cotangent = lax.optimization_barrier((parts, cotangent))
    arrivals = exchange(parts, ROW).reshape(ROWS * few, features)

    hidden_part = rows_times(cotangent, down_weight).astype(BF16)
    gate_got, up_got = swapped_half(gate_late), swapped_half(up_late)
    own, got = near_exchange(hidden_part.reshape(Z, -1, quarter))
    got[0], arrivals = lax.optimization_barrier((got[0], arrivals))
    sent = forward_products(core, arrivals, gate_weight, gate_got, up_weight, up_got)
    got[1], sent = lax.optimization_barrier((got[1], sent))
    hidden_sum = far_exchange(own, got)
    hidden_sum = hidden_sum.reshape(2, -1, quarter)
    hidden_keep = lax.dynamic_index_in_dim(hidden_sum, at_core, 0, keepdims=False)
    hidden_send = lax.dynamic_index_in_dim(hidden_sum, 1 - at_core, 0, keepdims=False)
    hidden_sum = paired(at_core, hidden_keep, lax.ppermute(hidden_send, "core", SWAP))
    grad_hidden = lax.ppermute(hidden_sum, EVERY, TO_OWNER)

    terms = exchange(sent.reshape(CHIPS, -1, units), PLANE)
    factors, hidden_keep, hidden_send = activations(core, terms)
    copies = unit_grads(core, factors, grad_hidden, CHIPS)
    hidden = paired(at_core, hidden_keep, lax.ppermute(hidden_send, "core", SWAP))
    hidden = gather_hidden(hidden).reshape(CHIPS, -1, quarter)
    pieces = exchange(copies, PLANE).reshape(-1, units)
    parts = token_products(core, pieces, gate_weight, gate_got, up_weight, up_got)
    parts = exchange(parts.reshape(ROWS, few, features), ROW)
    gate_grad, up_grad, gate_send, up_send = weight_grads(core, arrivals, pieces, depth)
    parts, hidden, gate_send = lax.optimization_barrier((parts, hidden, gate_send))
    hidden_panel = exchange(hidden, PLANE).reshape(-1, quarter)

    terms = parts.reshape(CHIPS, CORES, few, features).astype(F32)
    terms = jnp.sum(terms, axis=1).astype(BF16).reshape(Z, 2, few, features)
    terms = terms.transpose(0, 2, 1, 3).reshape(Z, few, width)
    own, got = near_exchange(terms)

    output = times(hidden_panel, down_weight).astype(BF16).reshape(ROWS, few, width)
    output = exchange(output, ROW)
    grad_tokens = far_exchange(own, got)

    gate_back = lax.ppermute(gate_send, "core", SWAP)
    up_back = lax.ppermute(up_send, "core", SWAP)
    gate_grad, up_grad = fill(core, gate_grad, up_grad, gate_back, up_back)
    grad_down_weight = columns_times(hidden_panel, cotangent).astype(BF16)
    output, grad_tokens, gate_grad, up_grad, grad_down_weight = lax.optimization_barrier(
        (output, grad_tokens, gate_grad, up_grad, grad_down_weight)
    )
    output = total(output).astype(BF16)
    return output, grad_tokens, gate_grad, up_grad, grad_down_weight


def solution(mesh):
    fine = Mesh(mesh.devices.reshape(Y, X, CORES, Z), EVERY)
    spec = P(ROW, "z")
    return jax.shard_map(
        local, mesh=fine, in_specs=(spec,) * 5, out_specs=(spec,) * 5, check_vma=False
    )
```

```python
import jax
import jax.numpy as jnp
from jax import lax
from jax.experimental import pallas as pl
from jax.experimental.pallas import tpu as pltpu
from jax.sharding import Mesh, PartitionSpec as P

Y, X, CORES, Z = 4, 4, 2, 8
CHIPS = Y * X
ROWS = CHIPS * CORES
PLANE = ("y", "x")
ROW = ("y", "x", "core")
EVERY = ("y", "x", "core", "z")
SWAP = [(0, 1), (1, 0)]
BF16, F32 = jnp.bfloat16, jnp.float32
VMEM_LIMIT = 48 * 1024 * 1024


def rows_times(left, right):
    return lax.dot_general(left, right, (((1,), (1,)), ((), ())), preferred_element_type=F32)


def columns_times(left, right):
    return lax.dot_general(left, right, (((0,), (0,)), ((), ())), preferred_element_type=F32)


def times(left, right):
    return jnp.dot(left, right, preferred_element_type=F32)


def exchange(blocks, axis):
    return lax.all_to_all(blocks, axis, split_axis=0, concat_axis=0, tiled=True)


def total(blocks):
    return jnp.sum(blocks.astype(F32), axis=0)


def pairs(distance):
    return [(z, z ^ distance) for z in range(Z)]


def paired(at_core, own, got):
    return jnp.where(at_core == 0, jnp.stack([own, got]), jnp.stack([got, own]))


def gather_columns(block, late=()):
    z = lax.axis_index("z")
    share = block[None, None, None]
    for axis, distance in enumerate((4, 2, 1)):
        got = lax.ppermute(share, "z", pairs(distance))
        if axis == 0 and late:
            got, *late = lax.optimization_barrier((got, *late))
        low = (z // distance) % 2 == 0
        share = jnp.where(
            low, jnp.concatenate([share, got], axis), jnp.concatenate([got, share], axis)
        )
    share = share.reshape((Z,) + block.shape)
    return (share, *late) if late else share


def near_order(z, near):
    near = [jnp.where(z % 2 == 0, near[at], near[at ^ 1]) for at in range(4)]
    return [jnp.where(z // 2 % 2 == 0, near[at], near[at ^ 2]) for at in range(4)]


def gather_hidden(block):
    z = lax.axis_index("z")
    got = lax.ppermute(block, "z", pairs(4))
    low = z < 4
    share = jnp.where(low, jnp.stack([block, got]), jnp.stack([got, block]))
    near = [share] + [lax.ppermute(share, "z", pairs(distance)) for distance in (1, 2, 3)]
    return jnp.stack(near_order(z, near), 1).reshape((Z,) + block.shape)


def near_exchange(blocks):
    z = lax.axis_index("z")
    share = blocks.reshape((2, 4) + blocks.shape[1:])
    near = [
        lax.dynamic_index_in_dim(share, (z % 4) ^ distance, 1, keepdims=False)
        for distance in range(4)
    ]
    return near[0], [lax.ppermute(near[d], "z", pairs(d)) for d in (1, 2, 3)]


def far_exchange(own, got):
    z = lax.axis_index("z")
    share = own.astype(F32)
    for term in got:
        share = share + term.astype(F32)
    share = share.astype(BF16)
    keep = lax.dynamic_index_in_dim(share, z // 4, 0, keepdims=False)
    send = lax.dynamic_index_in_dim(share, 1 - z // 4, 0, keepdims=False)
    far = lax.ppermute(send, "z", pairs(4))
    return (keep.astype(F32) + far.astype(F32)).astype(BF16)


def owner_route():
    route = []
    for chip in range(CHIPS):
        for core in range(CORES):
            for z in range(Z):
                source = (chip * CORES + core) * Z + z
                target = ((2 * z + core) * CORES + chip % 2) * Z + chip // 2
                route.append((source, target))
    return route


TO_OWNER = owner_route()


def in_hbm(array):
    return pltpu.with_memory_space_constraint(array, pltpu.HBM)


def call(body, core, arrays, in_specs, out_shapes, out_specs, steps, scratch=(), aliases=None, cost=0):
    moved = sum(a.size * a.dtype.itemsize for a in arrays)
    return pl.pallas_call(
        body,
        grid_spec=pltpu.PrefetchScalarGridSpec(
            num_scalar_prefetch=1,
            grid=(steps,),
            in_specs=in_specs,
            out_specs=out_specs,
            scratch_shapes=list(scratch),
        ),
        out_shape=out_shapes,
        input_output_aliases=aliases or {},
        cost_estimate=pl.CostEstimate(flops=cost, bytes_accessed=moved, transcendentals=0),
        compiler_params=pltpu.CompilerParams(vmem_limit_bytes=VMEM_LIMIT),
    )(core, *arrays)


def my_columns(step, core, *_):
    return (0, 2 * core[0] + step)


def your_columns(step, core, *_):
    return (0, 2 * (1 - core[0]) + step)


def in_turn(step, *_):
    return (0, step)


def panels(core, panel_ref, depth):
    first, second = panel_ref[:, :depth], panel_ref[:, depth:]
    own = core[0] == 0
    return jnp.where(own, first, second), jnp.where(own, second, first)


def forward_products(core, arrivals, gate_weight, gate_got, up_weight, up_got):
    rows, depth = arrivals.shape[0], gate_weight.shape[0]
    quarter = gate_weight.shape[1] // 4

    def body(core, panel, gate_mine, gate_other, up_mine, up_other, out):
        mine, other = panels(core, panel, depth)
        gate = times(mine, gate_mine[...]) + times(other, gate_other[...])
        out[:, :quarter] = gate.astype(BF16)
        up = times(mine, up_mine[...]) + times(other, up_other[...])
        out[:, quarter:] = up.astype(BF16)

    weight = pl.BlockSpec((depth, quarter), my_columns)
    got = pl.BlockSpec((depth, quarter), in_turn)
    return call(
        body,
        core,
        (arrivals, in_hbm(gate_weight), gate_got, in_hbm(up_weight), up_got),
        [pl.BlockSpec((rows, 2 * depth), lambda step, core: (0, 0)), weight, got, weight, got],
        pltpu.HBM((rows, 4 * quarter), BF16),
        pl.BlockSpec((rows, 2 * quarter), in_turn),
        2,
        cost=16 * rows * depth * quarter,
    )


def activations(core, terms):
    chips, tall, wide = terms.shape
    quarter = wide // 4

    def body(core, terms, factors, keep, send):
        both = terms[0].astype(F32)
        for chip in range(1, chips):
            both = both + terms[chip].astype(F32)
        gate, up = both[:, :quarter], both[:, quarter:]
        sigmoid_gate = 1.0 / (1.0 + jnp.exp(-gate))
        silu_gate = gate * sigmoid_gate
        factors[:, :quarter] = up * sigmoid_gate * (1.0 + gate * (1.0 - sigmoid_gate))
        factors[:, quarter:] = silu_gate
        hidden = (silu_gate * up).astype(BF16)

        @pl.when(pl.program_id(0) == core[0])
        def _():
            keep[...] = hidden

        @pl.when(pl.program_id(0) != core[0])
        def _():
            send[...] = hidden

    half = pl.BlockSpec((chips, tall, 2 * quarter), lambda step, core: (0, 0, step))
    flat = pl.BlockSpec((tall, quarter), lambda step, core: (0, 0))
    return call(
        body,
        core,
        (terms,),
        [half],
        [jax.ShapeDtypeStruct((tall, wide), F32)]
        + [jax.ShapeDtypeStruct((tall, quarter), BF16)] * 2,
        [pl.BlockSpec((tall, 2 * quarter), in_turn), flat, flat],
        2,
        cost=30 * tall * wide,
    )


def unit_grads(core, factors, grad_hidden, chips):
    tall, wide = factors.shape
    quarter = wide // 4

    def body(core, factors, grad_hidden, copies):
        cotangent = grad_hidden[0].astype(F32)
        grad_gate = (cotangent * factors[:, :quarter]).astype(BF16)
        grad_up = (cotangent * factors[:, quarter:]).astype(BF16)
        for chip in range(chips):
            copies[chip, :, :quarter] = grad_gate
            copies[chip, :, quarter:] = grad_up

    return call(
        body,
        core,
        (factors, grad_hidden),
        [
            pl.BlockSpec((tall, 2 * quarter), in_turn),
            pl.BlockSpec((1, tall, quarter), lambda step, core: (step, 0, 0)),
        ],
        pltpu.HBM((chips, tall, wide), BF16),
        pl.BlockSpec((chips, tall, 2 * quarter), lambda step, core: (0, 0, step)),
        2,
        cost=2 * tall * wide,
    )


def token_products(core, pieces, gate_weight, gate_got, up_weight, up_got):
    depth = gate_weight.shape[0]
    rows, half = pieces.shape[0], pieces.shape[1] // 2
    quarter = half // 2

    def body(core, piece, gate_mine, gate_other, up_mine, up_other, out, mine, other):
        piece_gate, piece_up = piece[:, :quarter], piece[:, quarter:]
        term_mine = rows_times(piece_gate, gate_mine[...]) + rows_times(piece_up, up_mine[...])
        term_other = rows_times(piece_gate, gate_other[...]) + rows_times(piece_up, up_other[...])

        @pl.when(pl.program_id(0) == 0)
        def _():
            mine[...] = term_mine
            other[...] = term_other

        @pl.when(pl.program_id(0) == 1)
        def _():
            sum_mine = (mine[...] + term_mine).astype(BF16)
            sum_other = (other[...] + term_other).astype(BF16)
            own = core[0] == 0
            out[:, :depth] = jnp.where(own, sum_mine, sum_other)
            out[:, depth:] = jnp.where(own, sum_other, sum_mine)

    weight = pl.BlockSpec((depth, quarter), my_columns)
    got = pl.BlockSpec((depth, quarter), in_turn)
    return call(
        body,
        core,
        (pieces, in_hbm(gate_weight), gate_got, in_hbm(up_weight), up_got),
        [
            pl.BlockSpec((rows, half), in_turn),
            weight,
            got,
            weight,
            got,
        ],
        jax.ShapeDtypeStruct((rows, 2 * depth), BF16),
        pl.BlockSpec((rows, 2 * depth), lambda step, core: (0, 0)),
        2,
        scratch=[pltpu.VMEM((rows, depth), F32)] * 2,
        cost=16 * rows * depth * quarter,
    )


def weight_grads(core, arrivals, pieces, depth):
    rows = arrivals.shape[0]
    wide = pieces.shape[1] // 2
    quarter = wide // 2

    def body(core, panel, piece, gate_grad, up_grad, gate_send, up_send):
        mine, other = panels(core, panel, depth)
        piece_gate, piece_up = piece[:, :quarter], piece[:, quarter:]
        gate_send[...] = columns_times(other, piece_gate).astype(BF16)
        up_send[...] = columns_times(other, piece_up).astype(BF16)
        gate_grad[...] = columns_times(mine, piece_gate).astype(BF16)
        up_grad[...] = columns_times(mine, piece_up).astype(BF16)

    mine = pl.BlockSpec((depth, quarter), my_columns)
    send = pl.BlockSpec((depth, quarter), in_turn)
    return call(
        body,
        core,
        (arrivals, pieces),
        [
            pl.BlockSpec((rows, 2 * depth), lambda step, core: (0, 0)),
            pl.BlockSpec((rows, wide), in_turn),
        ],
        [jax.ShapeDtypeStruct((depth, 4 * quarter), BF16)] * 2
        + [jax.ShapeDtypeStruct((depth, 2 * quarter), BF16)] * 2,
        [mine, mine, send, send],
        2,
        cost=16 * rows * depth * quarter,
    )


def fill(core, gate_grad, up_grad, gate_got, up_got):
    depth, units = gate_grad.shape
    quarter = units // 4

    def body(core, _, __, gate_got, up_got, gate_out, up_out):
        gate_out[...] = gate_got[...]
        up_out[...] = up_got[...]

    anywhere = pl.BlockSpec(memory_space=pl.ANY)
    got = pl.BlockSpec((depth, quarter), in_turn)
    out = pl.BlockSpec((depth, quarter), your_columns)
    return call(
        body,
        core,
        (gate_grad, up_grad, gate_got, up_got),
        [anywhere, anywhere, got, got],
        [jax.ShapeDtypeStruct(gate_grad.shape, BF16)] * 2,
        [out, out],
        2,
        aliases={1: 0, 2: 1},
    )


def local(tokens, gate_weight, up_weight, down_weight, out_grad):
    at_core = lax.axis_index("core")
    core = at_core.astype(jnp.int32).reshape(1)
    few, width = tokens.shape
    depth, units = gate_weight.shape
    half, quarter = units // 2, units // 4

    def swapped_half(weight):
        theirs = lax.dynamic_slice_in_dim(weight, (1 - at_core) * half, half, 1)
        return lax.ppermute(theirs, "core", SWAP)

    features = 2 * depth
    copies = jnp.broadcast_to(out_grad[None], (ROWS, few, width))
    cotangent = exchange(copies, ROW).reshape(ROWS * few, width)

    parts, gate_late, up_late = gather_columns(tokens, (gate_weight, up_weight))
    parts = parts.reshape(Z, few, 2, features).transpose(0, 2, 1, 3)
    parts = parts.reshape(CHIPS, 1, few, features)
    parts = jnp.broadcast_to(parts, (CHIPS, CORES, few, features))
    parts = parts.reshape(ROWS, few, features)
    parts, cotangent = lax.optimization_barrier((parts, cotangent))
    arrivals = exchange(parts, ROW).reshape(ROWS * few, features)

    hidden_part = rows_times(cotangent, down_weight).astype(BF16)
    gate_got, up_got = swapped_half(gate_late), swapped_half(up_late)
    own, got = near_exchange(hidden_part.reshape(Z, -1, quarter))
    got[0], arrivals = lax.optimization_barrier((got[0], arrivals))
    sent = forward_products(core, arrivals, gate_weight, gate_got, up_weight, up_got)
    got[1], sent = lax.optimization_barrier((got[1], sent))
    hidden_sum = far_exchange(own, got)
    hidden_sum = hidden_sum.reshape(2, -1, quarter)
    hidden_keep = lax.dynamic_index_in_dim(hidden_sum, at_core, 0, keepdims=False)
    hidden_send = lax.dynamic_index_in_dim(hidden_sum, 1 - at_core, 0, keepdims=False)
    hidden_sum = paired(at_core, hidden_keep, lax.ppermute(hidden_send, "core", SWAP))
    grad_hidden = lax.ppermute(hidden_sum, EVERY, TO_OWNER)

    terms = exchange(sent.reshape(CHIPS, -1, units), PLANE)
    factors, hidden_keep, hidden_send = activations(core, terms)
    copies = unit_grads(core, factors, grad_hidden, CHIPS)
    hidden = paired(at_core, hidden_keep, lax.ppermute(hidden_send, "core", SWAP))
    hidden = gather_hidden(hidden).reshape(CHIPS, -1, quarter)
    pieces = exchange(copies, PLANE).reshape(-1, units)
    parts = token_products(core, pieces, gate_weight, gate_got, up_weight, up_got)
    parts = exchange(parts.reshape(ROWS, few, features), ROW)
    gate_grad, up_grad, gate_send, up_send = weight_grads(core, arrivals, pieces, depth)
    parts, hidden, gate_send = lax.optimization_barrier((parts, hidden, gate_send))
    hidden_panel = exchange(hidden, PLANE).reshape(-1, quarter)

    terms = parts.reshape(CHIPS, CORES, few, features).astype(F32)
    terms = jnp.sum(terms, axis=1).astype(BF16).reshape(Z, 2, few, features)
    terms = terms.transpose(0, 2, 1, 3).reshape(Z, few, width)
    own, got = near_exchange(terms)

    output = times(hidden_panel, down_weight).astype(BF16).reshape(ROWS, few, width)
    own, output = lax.optimization_barrier((own, output))
    output = exchange(output, ROW)
    grad_tokens = far_exchange(own, got)

    gate_back = lax.ppermute(gate_send, "core", SWAP)
    up_back = lax.ppermute(up_send, "core", SWAP)
    gate_grad, up_grad = fill(core, gate_grad, up_grad, gate_back, up_back)
    grad_down_weight = columns_times(hidden_panel, cotangent).astype(BF16)
    output, grad_tokens, gate_grad, up_grad, grad_down_weight = lax.optimization_barrier(
        (output, grad_tokens, gate_grad, up_grad, grad_down_weight)
    )
    output = total(output).astype(BF16)
    return output, grad_tokens, gate_grad, up_grad, grad_down_weight


def solution(mesh):
    fine = Mesh(mesh.devices.reshape(Y, X, CORES, Z), EVERY)
    spec = P(ROW, "z")
    return jax.shard_map(
        local, mesh=fine, in_specs=(spec,) * 5, out_specs=(spec,) * 5, check_vma=False
    )
```
